256 devices in a mesh: gx: 8 (over z), gy: 8 (over x, core), gz: 4 (over y).
Axes of the slice: x: 4, y: 4, z: 8, core: 2. Of those that a mesh axis runs over, the one named last changes fastest.
Arguments:
- right_side: float32 [5, 64, 16, 2048], P(None, 'gx', 'gz', 'gy'), may hold values from -6 to 6
- conductance: float32 [64, 16, 2048], P('gx', 'gz', 'gy'), may hold values from 0.5 to 1
- blocks: float32 [27, 5, 5], replicated, may hold values from -0.3125 to 0.3125
Outputs:
- solution: float32 [5, 64, 16, 2048], P(None, 'gx', 'gz', 'gy')
- residual: float32 [5, 64, 16, 2048], P(None, 'gx', 'gz', 'gy')
The draws below stay inside these ranges and needn't reach their ends.
All inputs are finite; a program needn't handle non-finite values.
Results may differ from the reference program's by a relative error of at most 0.00045.
Values sent between devices are 32-bit elements; how exact they have to be, the bound alone decides.
No kernel may reach another device: no remote copies, remote signals or barrier semaphores. Data moves between devices by JAX's collectives and lax.ppermute only.
A program may use at most 192 MiB of HBM per device.

```python
import math
import jax
import jax.numpy as jnp
from jax import lax

VARIABLES = 5
OFFSETS = 27
BASIS_STEPS = 4
CYCLES = 2
NX = 64
NZ = 16
NY = 2048


def level_of(own_key, extent, pieces, low, high):
    level, own = 1.0, jax.random.fold_in(own_key, 6)
    for axis_at, blocks in pieces:
        steps = jnp.exp(jax.random.uniform(jax.random.fold_in(own, axis_at), (blocks,), jnp.float32, low / len(pieces), high / len(pieces)))
        level = level * jnp.repeat(steps, extent[axis_at] // blocks).reshape([-1 if axis == axis_at else 1 for axis in range(len(extent))])
    return level


def scatter_about(own_key, dims, spread, most, pieces=(), dtype=jnp.bfloat16):
    result = jax.random.normal(own_key, dims, jnp.float32) * spread
    if len(pieces) > 0:
        result = level_of(own_key, dims, pieces, -0.22, 0.18) * result
    return jnp.clip(result, min=-most, max=most).astype(dtype)


def setup_inputs(seed: int = 0) -> dict:
    arg_keys = jax.random.split(jax.random.key(seed), 4)
    return {
        "right_side": scatter_about(arg_keys[0], (VARIABLES, NX, NZ, NY), 1.0, 6.0, ((1, 8), (2, 4), (3, 8)), jnp.float32),
        "conductance": jnp.clip(jnp.exp(math.log(1.0) - 0.6931472 * jax.random.uniform(arg_keys[1], (NX, NZ, NY), jnp.float32) ** level_of(arg_keys[1], (NX, NZ, NY), ((0, 8), (1, 4), (2, 8)), -0.2, 0.2)), 0.5, 1.0),
        "blocks": scatter_about(arg_keys[2], (OFFSETS, VARIABLES, VARIABLES), 400 ** -0.5, 0.3125, (), jnp.float32),
    }


precise = lax.Precision.HIGHEST

def couple(field, conductance, blocks):
    padded = jnp.pad(field, ((0, 0), (1, 1), (1, 1), (1, 1)))
    cond_pad = jnp.pad(conductance, 1)
    extent_x, extent_z, extent_y = conductance.shape
    total = jnp.zeros(field.shape, jnp.float32)
    for along_x in range(3):
        for along_z in range(3):
            for along_y in range(3):
                offset = 9 * along_x + 3 * along_z + along_y
                near_cond = cond_pad[along_x:along_x + extent_x, along_z:along_z + extent_z, along_y:along_y + extent_y]
                near_field = padded[:, along_x:along_x + extent_x, along_z:along_z + extent_z, along_y:along_y + extent_y]
                total = total + jnp.einsum('ij,jabc->iabc', blocks[offset], near_cond * near_field, precision=precise)
    return conductance * total

def solve_small(gram):
    paired = gram[:-1, :] + gram[1:, :]
    normal = paired[:, :-1] + paired[:, 1:]
    target = paired[:, 0]
    lower = jnp.linalg.cholesky(normal)
    count = normal.shape[0]
    forward = []
    for row_at in range(count):
        value = target[row_at]
        for col_at in range(row_at):
            value = value - lower[row_at, col_at] * forward[col_at]
        forward.append(value / lower[row_at, row_at])
    backward = [None] * count
    for row_at in range(count - 1, -1, -1):
        value = forward[row_at]
        for col_at in range(row_at + 1, count):
            value = value - lower[col_at, row_at] * backward[col_at]
        backward[row_at] = value / lower[row_at, row_at]
    return backward

def update(solution, basis, coefs):
    steps_count = len(coefs)
    for step_at in range(steps_count):
        solution = solution + coefs[step_at] * basis[step_at]
    residual = (1.0 - coefs[0]) * basis[0]
    for step_at in range(1, steps_count):
        residual = residual - (coefs[step_at - 1] + coefs[step_at]) * basis[step_at]
    residual = residual - coefs[steps_count - 1] * basis[steps_count]
    return (solution, residual)

def reference(right_side, conductance, blocks):
    solution = jnp.zeros(right_side.shape, jnp.float32)
    residual = right_side
    for cycle_at in range(CYCLES):
        basis = [residual]
        for power_at in range(BASIS_STEPS):
            basis.append(couple(basis[-1], conductance, blocks))
        rows_list = []
        for left_at in range(BASIS_STEPS + 1):
            rows_list.append(jnp.stack([jnp.sum(basis[left_at] * basis[right_at]) for right_at in range(BASIS_STEPS + 1)]))
        gram = jnp.stack(rows_list)
        coefs = solve_small(gram)
        solution, residual = update(solution, basis, coefs)
    return (solution, residual)
```

```python
import functools

import jax
import jax.numpy as jnp
from jax import lax
from jax.experimental import pallas as pl
from jax.experimental.pallas import tpu as pltpu
from jax.sharding import PartitionSpec as P

STEPS = 4
POWERS = 2 * STEPS
VARS = 5
HALO = POWERS
LANES = 128
OWN = 8
WIDE = OWN + 2 * HALO
PAIRS = [(i, j) for i in range(POWERS + 1) for j in range(i, POWERS + 1)]

F32 = jnp.float32
BF16 = jnp.bfloat16
VMEM = 64 * 1024 * 1024 * 7 // 8


def lane_iota(rows):
    return lax.broadcasted_iota(jnp.int32, (rows, LANES), 1)


def roll_lanes(value, shift):
    shift = shift % LANES
    return value if shift == 0 else pltpu.roll(value, shift, value.ndim - 1)


def pack_kernel(peers, own_ref, left_ref, right_ref, out_ref):
    fields, extent_z, rows, _ = own_ref.shape
    lanes = lane_iota(rows)
    for peer in range(peers):
        start = LANES + OWN * peer - HALO
        tile, offset = start // LANES, start % LANES

        def strip(field, z_at, place):
            def part(tile_at):
                if tile_at == 0:
                    whole = left_ref[field, z_at]
                elif tile_at == 3:
                    whole = right_ref[field, z_at]
                else:
                    whole = own_ref[field, z_at, :, LANES * (tile_at - 1) : LANES * tile_at]
                return roll_lanes(whole, place - offset)

            value = part(tile)
            if offset + WIDE > LANES:
                value = jnp.where(lanes < place + LANES - offset, value, part(tile + 1))
            return value

        for z_at in range(extent_z):
            total = jnp.zeros((rows, LANES), F32)
            for var in range(VARS):
                place = var * WIDE
                inside = (lanes >= place) & (lanes < place + WIDE)
                total = jnp.where(inside, strip(var, z_at, place), total)
            out_ref[peer, z_at] = total
        total = jnp.zeros((rows, LANES), F32)
        for z_at in range(extent_z):
            place = z_at * WIDE
            inside = (lanes >= place) & (lanes < place + WIDE)
            total = jnp.where(inside, strip(VARS, z_at, place), total)
        out_ref[peer, extent_z] = total


def powers_kernel(count_x, count_z, chunk, in_ref, rows_ref, basis_ref, gram_ref, pieces, matrix, cond):
    extent_z, rows = in_ref.shape[1] - 1, in_ref.shape[2]
    size_z, size_x = extent_z * count_z, rows * count_x

    row_at = lax.broadcasted_iota(jnp.int32, (WIDE, LANES), 0)
    lane_at = lax.broadcasted_iota(jnp.int32, (WIDE, LANES), 1)
    ahead = jnp.where(lane_at < VARS * WIDE, row_at - lane_at % WIDE, 2 * LANES)
    for along_x in range(3):
        for along_z in range(3):
            groups = []
            for source in range(VARS):
                total = jnp.zeros((WIDE, LANES), F32)
                for along_y in range(3):
                    line = (9 * along_x + 3 * along_z + along_y) * VARS + source
                    row = rows_ref[line : line + 1, :]
                    total = jnp.where(ahead == along_y - 1, row, total)
                groups.append(total)
            groups.append(jnp.zeros((LANES - VARS * WIDE, LANES), F32))
            whole = jnp.concatenate(groups, axis=0)
            high = whole.astype(BF16)
            low = (whole - high.astype(F32)).astype(BF16)
            columns = slice(along_x * LANES, (along_x + 1) * LANES)
            base = along_z * 2 * LANES
            matrix[base : base + LANES, columns] = high
            matrix[base + LANES : base + 2 * LANES, columns] = high
            base = 6 * LANES + along_z * LANES
            matrix[base : base + LANES, columns] = low

    def keep(slot, z_from, value):
        high = value.astype(BF16)
        low = (value - high.astype(F32)).astype(BF16)
        pieces[slot, pl.ds(z_from + 1, value.shape[0]), :, :LANES] = high
        pieces[slot, pl.ds(z_from + 1, value.shape[0]), :, LANES:] = low

    for slot in range(2):
        for edge in (0, size_z + 1):
            pieces[slot, edge] = jnp.zeros((size_x, 2 * LANES), BF16)

    lanes = lane_iota(rows)
    for group_z in range(count_z):
        for z_local in range(extent_z):
            z_at = group_z * extent_z + z_local
            conds, fields = [], []
            for group_x in range(count_x):
                peer = group_x * count_z + group_z
                packed = in_ref[peer, extent_z]
                total = jnp.zeros((rows, LANES), F32)
                for var in range(VARS):
                    inside = (lanes >= var * WIDE) & (lanes < (var + 1) * WIDE)
                    total = jnp.where(inside, roll_lanes(packed, (var - z_local) * WIDE), total)
                conds.append(total)
                fields.append(in_ref[peer, z_local])
            total = jnp.concatenate(conds, axis=0)
            field = jnp.concatenate(fields, axis=0)
            cond[z_at] = total
            basis_ref[0, z_at] = field
            keep(0, z_at, (total * field)[None])

    x_at = lax.broadcasted_iota(jnp.int32, (chunk, size_x, LANES), 1)

    def step(power, carry):
        now, later = (power + 1) % 2, power % 2
        for z_from in range(0, size_z, chunk):
            near = [pieces[now, z_from + dz : z_from + dz + chunk] for dz in range(3)]
            stacked = jnp.concatenate(near + [value[:, :, :LANES] for value in near], axis=-1)
            stacked = stacked.reshape(chunk * size_x, 9 * LANES)
            product = jnp.dot(stacked, matrix[...], preferred_element_type=F32)
            product = product.reshape(chunk, size_x, 3 * LANES)
            before = pltpu.roll(product[:, :, :LANES], 1, 1)
            after = pltpu.roll(product[:, :, 2 * LANES :], size_x - 1, 1)
            total = product[:, :, LANES : 2 * LANES]
            total = total + jnp.where(x_at > 0, before, 0.0)
            total = total + jnp.where(x_at < size_x - 1, after, 0.0)
            weight = cond[z_from : z_from + chunk]
            value = weight * total
            basis_ref[power, z_from : z_from + chunk] = value
            keep(later, z_from, weight * value)
        return carry

    lax.fori_loop(1, POWERS + 1, step, 0)

    def add(z_at, sums):
        for group_x in range(count_x):
            tiles = [
                basis_ref[power, z_at, group_x * rows : (group_x + 1) * rows, :] for power in range(POWERS + 1)
            ]
            sums = tuple(total + tiles[i] * tiles[j] for total, (i, j) in zip(sums, PAIRS))
        return sums

    sums = lax.fori_loop(0, size_z, add, tuple(jnp.zeros((rows, LANES), F32) for _ in PAIRS))
    lines = [jnp.sum(total, axis=0, keepdims=True) for total in sums]
    lines.append(jnp.zeros((LANES - len(PAIRS), LANES), F32))
    table = jnp.concatenate(lines, axis=0)
    inner = lane_iota(LANES) % WIDE
    table = jnp.where((inner >= HALO) & (inner < HALO + OWN) & (lane_iota(LANES) < VARS * WIDE), table, 0.0)
    gram_ref[...] = lax.dot_general(
        jnp.ones((8, LANES), F32),
        table,
        (((1,), (1,)), ((), ())),
        precision=lax.Precision.HIGHEST,
        preferred_element_type=F32,
    )


def solve(gram):
    paired = [[gram[i][j] + gram[i + 1][j] for j in range(STEPS + 1)] for i in range(STEPS)]
    normal = [[paired[i][j] + paired[i][j + 1] for j in range(STEPS)] for i in range(STEPS)]
    target = [paired[i][0] for i in range(STEPS)]
    lower = [[None] * STEPS for _ in range(STEPS)]
    inverse = []
    for col in range(STEPS):
        value = normal[col][col]
        for k in range(col):
            value = value - lower[col][k] * lower[col][k]
        root = jnp.sqrt(value)
        lower[col][col] = root
        inverse.append(1.0 / root)
        for row in range(col + 1, STEPS):
            value = normal[row][col]
            for k in range(col):
                value = value - lower[row][k] * lower[col][k]
            lower[row][col] = value * inverse[col]
    forward = []
    for row in range(STEPS):
        value = target[row]
        for col in range(row):
            value = value - lower[row][col] * forward[col]
        forward.append(value * inverse[row])
    coefs = [None] * STEPS
    for row in range(STEPS - 1, -1, -1):
        value = forward[row]
        for col in range(row + 1, STEPS):
            value = value - lower[col][row] * coefs[col]
        coefs[row] = value * inverse[row]
    return coefs


def remainder(coefs):
    inner = [-(coefs[k - 1] + coefs[k]) for k in range(1, STEPS)]
    return [1.0 - coefs[0]] + inner + [-coefs[STEPS - 1]]


def combine_kernel(count_x, count_z, grams_ref, basis_ref, out_ref):
    _, size_z, size_x, _ = basis_ref.shape
    rows, extent_z = size_x // count_x, size_z // count_z
    line = jnp.sum(grams_ref[...], axis=0, keepdims=True)
    where = lane_iota(1)
    entry = {}
    for at, (i, j) in enumerate(PAIRS):
        value = jnp.sum(jnp.where(where == at, line, 0.0), axis=1, keepdims=True)
        entry[i, j] = entry[j, i] = value
    first = solve([[entry[i, j] for j in range(STEPS + 1)] for i in range(STEPS + 1)])
    left = remainder(first)
    half = {}
    for i in range(STEPS + 1):
        for j in range(POWERS + 1):
            value = left[0] * entry[i, j]
            for k in range(1, STEPS + 1):
                value = value + left[k] * entry[i + k, j]
            half[i, j] = value
    second_gram = []
    for i in range(STEPS + 1):
        line = []
        for j in range(STEPS + 1):
            value = left[0] * half[i, j]
            for k in range(1, STEPS + 1):
                value = value + left[k] * half[i, j + k]
            line.append(value)
        second_gram.append(line)
    second = solve(second_gram)
    last = remainder(second)
    of_solution = list(first) + [0.0] * STEPS
    of_residual = [0.0] * (POWERS + 1)
    for i in range(STEPS):
        for k in range(STEPS + 1):
            of_solution[i + k] = of_solution[i + k] + second[i] * left[k]
    for i in range(STEPS + 1):
        for k in range(STEPS + 1):
            of_residual[i + k] = of_residual[i + k] + last[i] * left[k]
    of_solution = [jnp.broadcast_to(value, (rows, LANES)) for value in of_solution]
    of_residual = [jnp.broadcast_to(value, (rows, LANES)) for value in of_residual]
    own = (lane_iota(rows) % WIDE) < HALO + OWN

    def each(z_at, carry):
        for group_x in range(count_x):
            tiles = [
                basis_ref[power, z_at, group_x * rows : (group_x + 1) * rows, :] for power in range(POWERS + 1)
            ]
            solution = of_solution[0] * tiles[0]
            residual = of_residual[0] * tiles[0]
            for power in range(1, POWERS + 1):
                residual = residual + of_residual[power] * tiles[power]
                if power < POWERS:
                    solution = solution + of_solution[power] * tiles[power]
            both = jnp.where(own, solution, roll_lanes(residual, OWN))
            out_ref[group_x * count_z + z_at // extent_z, z_at % extent_z] = both
        return carry

    lax.fori_loop(0, size_z, each, 0)


def unpack_kernel(in_ref, solution_ref, residual_ref):
    peers, extent_z, rows, _ = in_ref.shape
    lanes = lane_iota(rows)
    each = LANES // OWN
    for z_at in range(extent_z):
        for half in range(peers // each):
            for part, ref in enumerate((solution_ref, residual_ref)):
                for var in range(VARS):
                    total = None
                    for at in range(each):
                        value = in_ref[half * each + at, z_at]
                        value = roll_lanes(value, at * OWN - (var * WIDE + HALO + part * OWN))
                        total = value if total is None else jnp.where(lanes < at * OWN, total, value)
                    ref[var, z_at, :, half * LANES : (half + 1) * LANES] = total


def call(kernel, out_shape, scratch=()):
    return pl.pallas_call(
        kernel,
        out_shape=out_shape,
        scratch_shapes=scratch,
        compiler_params=pltpu.CompilerParams(vmem_limit_bytes=VMEM),
    )


def per_device(right_side, conductance, blocks):
    count_x, count_y, count_z = (lax.axis_size(axis) for axis in ("gx", "gy", "gz"))
    peers = count_x * count_z
    _, extent_x, extent_z, extent_y = right_side.shape
    size_x, size_z = extent_x * count_x, extent_z * count_z

    fields = jnp.concatenate([right_side, conductance[None]], axis=0).transpose(0, 2, 1, 3)
    up = [(i, i + 1) for i in range(count_y - 1)]
    down = [(i + 1, i) for i in range(count_y - 1)]
    left = lax.ppermute(fields[..., extent_y - LANES :], "gy", up)
    right = lax.ppermute(fields[..., :LANES], "gy", down)
    strips = call(
        functools.partial(pack_kernel, peers),
        jax.ShapeDtypeStruct((peers, extent_z + 1, extent_x, LANES), F32),
    )(fields, left, right)
    strips = lax.all_to_all(strips, ("gx", "gz"), 0, 0, tiled=True)

    rows = jnp.repeat(blocks.transpose(0, 2, 1).reshape(-1, VARS), WIDE, axis=1)
    rows = jnp.pad(rows, ((0, 1), (0, LANES - VARS * WIDE)))
    chunk = 4
    basis, gram = call(
        functools.partial(powers_kernel, count_x, count_z, chunk),
        (
            jax.ShapeDtypeStruct((POWERS + 1, size_z, size_x, LANES), F32),
            jax.ShapeDtypeStruct((8, LANES), F32),
        ),
        (
            pltpu.VMEM((2, size_z + 2, size_x, 2 * LANES), BF16),
            pltpu.VMEM((9 * LANES, 3 * LANES), BF16),
            pltpu.VMEM((size_z, size_x, LANES), F32),
        ),
    )(strips, rows)

    devices = peers * count_y
    grams = jnp.broadcast_to(gram[:1][None], (devices, 1, LANES))
    grams = lax.all_to_all(grams, ("gx", "gy", "gz"), 0, 0, tiled=True).reshape(devices, LANES)
    both = call(
        functools.partial(combine_kernel, count_x, count_z),
        jax.ShapeDtypeStruct((peers, extent_z, extent_x, LANES), F32),
    )(grams, basis)
    both = lax.all_to_all(both, ("gx", "gz"), 0, 0, tiled=True)
    shape = jax.ShapeDtypeStruct((VARS, extent_z, extent_x, extent_y), F32)
    solution, residual = call(unpack_kernel, (shape, shape))(both)
    return solution.transpose(0, 2, 1, 3), residual.transpose(0, 2, 1, 3)


def solution(mesh):
    in_specs = (P(None, "gx", "gz", "gy"), P("gx", "gz", "gy"), P())
    out_specs = (P(None, "gx", "gz", "gy"), P(None, "gx", "gz", "gy"))
    return jax.shard_map(
        per_device, mesh=mesh, in_specs=in_specs, out_specs=out_specs, check_vma=False
    )
```

```python
import functools

import jax
import jax.numpy as jnp
from jax import lax
from jax.experimental import pallas as pl
from jax.experimental.pallas import tpu as pltpu
from jax.sharding import PartitionSpec as P

STEPS = 4
POWERS = 2 * STEPS
VARS = 5
FIELDS = VARS + 1
HALO = POWERS
LANES = 128
CHUNK = 8
PAIRS = [(i, j) for i in range(POWERS + 1) for j in range(i, POWERS + 1)]

F32 = jnp.float32
BF16 = jnp.bfloat16
VMEM = 24 * 1024 * 1024


def lane_iota(rows, lanes=LANES):
    return lax.broadcasted_iota(jnp.int32, (rows, lanes), 1)


def row_iota(rows, lanes=LANES):
    return lax.broadcasted_iota(jnp.int32, (rows, lanes), 0)


def roll_lanes(value, shift):
    shift = shift % LANES
    return value if shift == 0 else pltpu.roll(value, shift, value.ndim - 1)


def pieces_of(value, count):
    pieces = []
    for at in range(count):
        piece = value.astype(BF16)
        pieces.append(piece)
        if at < count - 1:
            value = value - piece.astype(F32)
    return pieces


def pack_kernel(peers, fields_ref, cond_ref, out_ref, first_ref, last_ref, own):
    _, extent_x, extent_z, extent_y = fields_ref.shape
    half = extent_x // 2
    group = FIELDS * extent_z
    for x_at in range(extent_x):
        for field in range(FIELDS):
            base = (x_at % half) * group + field * extent_z
            rows = slice(base, base + extent_z)
            own[x_at // half, rows, :] = fields_ref[field, x_at] if field < VARS else cond_ref[x_at]
    blank = jnp.zeros((LANES - half * group, LANES), F32)
    gap = jnp.zeros((HALO, LANES), F32)
    width = extent_y // peers
    for part in range(2):
        turned = []
        for tile in range(extent_y // LANES):
            value = own[part, : half * group, tile * LANES : (tile + 1) * LANES]
            turned.append(jnp.concatenate([value, blank], axis=0).T)
        whole = jnp.concatenate([gap] + turned + [gap], axis=0)
        for peer in range(peers):
            out_ref[peer, part] = whole[peer * width : peer * width + width + 2 * HALO]
        first_ref[part] = whole[HALO : 2 * HALO]
        last_ref[part] = whole[extent_y : extent_y + HALO]


def powers_kernel(
    own_x, extent_z, before_ref, here_ref, after_ref, rows_ref, basis_ref, gram_ref, spread, matrix, even, odd, cond
):
    peers, parts, wide_y, _ = here_ref.shape
    size_z = peers * extent_z
    used = VARS * size_z
    group = FIELDS * extent_z
    half = own_x // parts
    wide_x = 3 * parts * half
    own_y = wide_y - 2 * HALO

    row, lane = row_iota(LANES, 2 * LANES), lane_iota(LANES, 2 * LANES)
    column = lane % LANES
    wanted = jnp.where(lane < LANES, column // size_z, VARS)
    source_z = (row // group) * extent_z + row % extent_z
    hit = ((row % group) // extent_z == wanted) & (source_z == column % size_z)
    hit = hit & (column < used) & (row < peers * group)
    pick = jnp.where(hit, 1.0, 0.0).astype(BF16)
    for at in range(3):
        spread[at * LANES : (at + 1) * LANES, :] = pick

    row_z = row_iota(size_z)
    lane_z = lane_iota(size_z)
    ahead = jnp.where(lane_z < used, row_z - lane_z % size_z, LANES)
    lanes = lane_iota(used)
    rest = used - (LANES - used)
    blocks = []
    for along_x in range(3):
        parts_y = []
        for along_y in range(3):
            groups = []
            for source in range(VARS):
                total = jnp.zeros((size_z, LANES), F32)
                for along_z in range(3):
                    line = (9 * along_x + 3 * along_z + along_y) * VARS + source
                    total = jnp.where(ahead == along_z - 1, rows_ref[line : line + 1, :], total)
                groups.append(total)
            parts_y.append(jnp.concatenate(groups, axis=0))
        first = jnp.where(lanes < used, parts_y[1], roll_lanes(parts_y[2], used))
        second = jnp.where(lanes < used, parts_y[0], roll_lanes(parts_y[2], 2 * used))
        second = jnp.where(lanes < used + used - (LANES - used), second, 0.0)
        blocks.append(jnp.concatenate([first, second], axis=1))
    blocks.append(jnp.zeros((2 * LANES - 3 * used, 2 * LANES), F32))
    high, low = pieces_of(jnp.concatenate(blocks, axis=0), 2)
    matrix[: 2 * LANES, :] = high
    matrix[2 * LANES : 4 * LANES, :] = high
    matrix[4 * LANES :, :] = low

    at_x, at_y, at_z = (lax.axis_index(axis) for axis in ("gx", "gy", "gz"))
    count_x, count_y = lax.axis_size("gx"), lax.axis_size("gy")
    column_y = row_iota(wide_y) + ((at_y * peers + at_z) * own_y - HALO)
    inside_y = (column_y >= 0) & (column_y < count_y * peers * own_y)
    lane = lane_iota(wide_y)
    for block, ref in enumerate((before_ref, here_ref, after_ref)):
        block_x = at_x + (block - 1)
        inside = inside_y & (block_x >= 0) & (block_x < count_x)
        for part in range(parts):
            tiles = [ref[peer, part] for peer in range(peers)]
            gathered = []
            for x_local in range(half):
                total = roll_lanes(tiles[0], -x_local * group)
                for peer in range(1, peers):
                    moved = roll_lanes(tiles[peer], (peer - x_local) * group)
                    total = jnp.where(lane < peer * group, total, moved)
                gathered.append(total)
            split = pieces_of(jnp.concatenate(gathered, axis=0), 3)
            result = jnp.dot(jnp.concatenate(split, axis=1), spread[...], preferred_element_type=F32)
            for x_local in range(half):
                x_at = (block * parts + part) * half + x_local
                rows = slice(x_local * wide_y, (x_local + 1) * wide_y)
                field = result[rows, :LANES]
                weight = jnp.where(inside, result[rows, LANES:], 0.0)
                cond[x_at] = weight
                even[x_at + 1] = weight * field
                if block == 1:
                    basis_ref[0, part * half + x_local] = field[HALO : HALO + own_y]

    def apply(power, now, later, x_from, count):
        near = [now[x_from + at] for at in range(count + 2)]
        firsts, seconds = [], []
        for at in range(count):
            middle = roll_lanes(near[at + 1], used)
            firsts.append(jnp.where(lane < used, near[at], middle))
            last = roll_lanes(near[at + 2], 2 * used)
            seconds.append(jnp.where(lane < 2 * used - LANES, middle, last))
        stacked = jnp.concatenate(
            [jnp.concatenate(firsts, axis=0), jnp.concatenate(seconds, axis=0)], axis=1
        )
        high, low = pieces_of(stacked, 2)
        product = jnp.dot(jnp.concatenate([high, low, high], axis=1), matrix[...], preferred_element_type=F32)
        for at in range(count):
            x_at = x_from + at
            left = product[at * wide_y : (at + 1) * wide_y, :LANES]
            right = product[at * wide_y : (at + 1) * wide_y, LANES:]
            ahead = jnp.where(lane < LANES - used, roll_lanes(left, -used), roll_lanes(right, -2 * used))
            total = left + pltpu.roll(right, 1, 0) + pltpu.roll(ahead, wide_y - 1, 0)
            weight = cond[x_at]
            value = weight * total
            if 0 <= x_at - own_x < own_x:
                basis_ref[power, x_at - own_x] = value[HALO : HALO + own_y]
            if power < POWERS:
                later[x_at + 1] = weight * value

    slots = (even, odd)
    for power in range(1, POWERS + 1):
        for x_from in range(power, wide_x - power, CHUNK):
            x_to = min(x_from + CHUNK, wide_x - power)
            apply(power, slots[(power + 1) % 2], slots[power % 2], x_from, x_to - x_from)

    def add(x_at, sums):
        for tile in range(own_y // 8):
            tiles = [basis_ref[power, x_at, tile * 8 : (tile + 1) * 8, :] for power in range(POWERS + 1)]
            sums = tuple(total + tiles[i] * tiles[j] for total, (i, j) in zip(sums, PAIRS))
        return sums

    sums = lax.fori_loop(0, own_x, add, tuple(jnp.zeros((8, LANES), F32) for _ in PAIRS))
    lines = [jnp.sum(total, axis=0, keepdims=True) for total in sums]
    lines.append(jnp.zeros((LANES - len(PAIRS), LANES), F32))
    table = jnp.concatenate(lines, axis=0)
    line = lax.dot_general(
        jnp.ones((8, LANES), F32),
        table,
        (((1,), (1,)), ((), ())),
        precision=lax.Precision.HIGHEST,
        preferred_element_type=F32,
    )[:1]
    gram_ref[...] = jnp.broadcast_to(line[None], gram_ref.shape)


def solve(gram):
    paired = [[gram[i][j] + gram[i + 1][j] for j in range(STEPS + 1)] for i in range(STEPS)]
    normal = [[paired[i][j] + paired[i][j + 1] for j in range(STEPS)] for i in range(STEPS)]
    target = [paired[i][0] for i in range(STEPS)]
    lower = [[None] * STEPS for _ in range(STEPS)]
    inverse = []
    for col in range(STEPS):
        value = normal[col][col]
        for k in range(col):
            value = value - lower[col][k] * lower[col][k]
        root = jnp.sqrt(value)
        lower[col][col] = root
        inverse.append(1.0 / root)
        for row in range(col + 1, STEPS):
            value = normal[row][col]
            for k in range(col):
                value = value - lower[row][k] * lower[col][k]
            lower[row][col] = value * inverse[col]
    forward = []
    for row in range(STEPS):
        value = target[row]
        for col in range(row):
            value = value - lower[row][col] * forward[col]
        forward.append(value * inverse[row])
    coefs = [None] * STEPS
    for row in range(STEPS - 1, -1, -1):
        value = forward[row]
        for col in range(row + 1, STEPS):
            value = value - lower[col][row] * coefs[col]
        coefs[row] = value * inverse[row]
    return coefs


def remainder(coefs):
    inner = [-(coefs[k - 1] + coefs[k]) for k in range(1, STEPS)]
    return [1.0 - coefs[0]] + inner + [-coefs[STEPS - 1]]


def combine_kernel(peers, grams_ref, basis_ref, out_ref, turned):
    _, own_x, own_y, _ = basis_ref.shape
    line = jnp.sum(grams_ref[...], axis=0)
    where = lane_iota(1)
    entry = {}
    for at, (i, j) in enumerate(PAIRS):
        value = jnp.sum(jnp.where(where == at, line, 0.0), axis=1, keepdims=True)
        entry[i, j] = entry[j, i] = value
    first = solve([[entry[i, j] for j in range(STEPS + 1)] for i in range(STEPS + 1)])
    left = remainder(first)
    half = {}
    for i in range(STEPS + 1):
        for j in range(POWERS + 1):
            value = left[0] * entry[i, j]
            for k in range(1, STEPS + 1):
                value = value + left[k] * entry[i + k, j]
            half[i, j] = value
    second_gram = []
    for i in range(STEPS + 1):
        line = []
        for j in range(STEPS + 1):
            value = left[0] * half[i, j]
            for k in range(1, STEPS + 1):
                value = value + left[k] * half[i, j + k]
            line.append(value)
        second_gram.append(line)
    second = solve(second_gram)
    last = remainder(second)
    of_solution = list(first) + [0.0] * STEPS
    of_residual = [0.0] * (POWERS + 1)
    for i in range(STEPS):
        for k in range(STEPS + 1):
            of_solution[i + k] = of_solution[i + k] + second[i] * left[k]
    for i in range(STEPS + 1):
        for k in range(STEPS + 1):
            of_residual[i + k] = of_residual[i + k] + last[i] * left[k]
    of_solution = [jnp.broadcast_to(value, (8, LANES)) for value in of_solution]
    of_residual = [jnp.broadcast_to(value, (8, LANES)) for value in of_residual]

    size_z = 16
    extent_z = size_z // peers
    for x_at in range(own_x):
        solutions, residuals = [], []
        for tile in range(own_y // 8):
            tiles = [basis_ref[power, x_at, tile * 8 : (tile + 1) * 8, :] for power in range(POWERS + 1)]
            solution = of_solution[0] * tiles[0]
            residual = of_residual[0] * tiles[0]
            for power in range(1, POWERS + 1):
                residual = residual + of_residual[power] * tiles[power]
                if power < POWERS:
                    solution = solution + of_solution[power] * tiles[power]
            solutions.append(solution)
            residuals.append(residual)
        turned[x_at] = jnp.concatenate(solutions + residuals, axis=0).T
        for peer in range(peers):
            for var in range(VARS):
                source = var * size_z + peer * extent_z
                place = (x_at * VARS + var) * extent_z
                out_ref[peer, place : place + extent_z, :] = turned[x_at, source : source + extent_z, :]


def unpack_kernel(in_ref, solution_ref, residual_ref):
    peers, _, _ = in_ref.shape
    _, extent_x, extent_z, extent_y = solution_ref.shape
    lanes = lane_iota(extent_z)
    half = LANES // 2
    for x_at in range(extent_x):
        for var in range(VARS):
            place = (x_at * VARS + var) * extent_z
            for tile in range(extent_y // LANES):
                first = in_ref[2 * tile, place : place + extent_z, :]
                second = in_ref[2 * tile + 1, place : place + extent_z, :]
                columns = slice(tile * LANES, (tile + 1) * LANES)
                solution_ref[var, x_at, :, columns] = jnp.where(lanes < half, first, roll_lanes(second, half))
                residual_ref[var, x_at, :, columns] = jnp.where(lanes < half, roll_lanes(first, half), second)


def call(kernel, out_shape, scratch=()):
    return pl.pallas_call(
        kernel,
        out_shape=out_shape,
        scratch_shapes=scratch,
        compiler_params=pltpu.CompilerParams(vmem_limit_bytes=VMEM),
    )


def ring(count):
    up = [(i, (i + 1) % count) for i in range(count)]
    return up, [(j, i) for i, j in up]


def per_device(right_side, conductance, blocks):
    count_x, count_y, count_z = (lax.axis_size(axis) for axis in ("gx", "gy", "gz"))
    _, extent_x, extent_z, extent_y = right_side.shape
    size_z = extent_z * count_z
    own_y = extent_y // count_z
    wide_y = own_y + 2 * HALO

    up, down = ring(count_y)
    edge = jax.ShapeDtypeStruct((2, HALO, LANES), F32)
    strips, first, last = call(
        functools.partial(pack_kernel, count_z),
        (jax.ShapeDtypeStruct((count_z, 2, wide_y, LANES), F32), edge, edge),
        (pltpu.VMEM((2, LANES, extent_y), F32),),
    )(right_side, conductance)
    left = lax.ppermute(last, "gy", up)
    right = lax.ppermute(first, "gy", down)
    strips = strips.at[0, :, :HALO].set(left).at[count_z - 1, :, wide_y - HALO :].set(right)
    here = lax.all_to_all(strips, "gz", 0, 0, tiled=True)
    up, down = ring(count_x)
    before = lax.ppermute(here, "gx", up)
    after = lax.ppermute(here, "gx", down)

    rows = jnp.repeat(blocks.transpose(0, 2, 1).reshape(-1, VARS), size_z, axis=1)
    rows = jnp.pad(rows, ((0, 1), (0, LANES - VARS * size_z)))
    devices = count_x * count_y * count_z
    basis, gram = call(
        functools.partial(powers_kernel, extent_x, extent_z),
        (
            jax.ShapeDtypeStruct((POWERS + 1, extent_x, own_y, LANES), F32),
            jax.ShapeDtypeStruct((devices, 1, LANES), F32),
        ),
        (
            pltpu.VMEM((3 * LANES, 2 * LANES), BF16),
            pltpu.VMEM((6 * LANES, 2 * LANES), BF16),
            pltpu.VMEM((3 * extent_x + 2, wide_y, LANES), F32),
            pltpu.VMEM((3 * extent_x + 2, wide_y, LANES), F32),
            pltpu.VMEM((3 * extent_x, wide_y, LANES), F32),
        ),
    )(before, here, after, rows)

    gram = lax.all_to_all(gram, ("gx", "gy", "gz"), 0, 0, tiled=True)
    both = call(
        functools.partial(combine_kernel, count_z),
        jax.ShapeDtypeStruct((count_z, extent_x * VARS * extent_z, LANES), F32),
        (pltpu.VMEM((extent_x, LANES, LANES), F32),),
    )(gram, basis)
    both = lax.all_to_all(both, "gz", 0, 0, tiled=True)
    shape = jax.ShapeDtypeStruct(right_side.shape, F32)
    return call(unpack_kernel, (shape, shape))(both)


def solution(mesh):
    in_specs = (P(None, "gx", "gz", "gy"), P("gx", "gz", "gy"), P())
    out_specs = (P(None, "gx", "gz", "gy"), P(None, "gx", "gz", "gy"))
    return jax.shard_map(
        per_device, mesh=mesh, in_specs=in_specs, out_specs=out_specs, check_vma=False
    )
```

```python
import functools

import jax
import jax.numpy as jnp
from jax import lax
from jax.experimental import pallas as pl
from jax.experimental.pallas import tpu as pltpu
from jax.sharding import PartitionSpec as P

STEPS = 4
POWERS = 2 * STEPS
VARS = 5
FIELDS = VARS + 1
HALO = POWERS
LANES = 128
CHUNK = 10
PAIRS = [(i, j) for i in range(POWERS + 1) for j in range(i, POWERS + 1)]

F32 = jnp.float32
BF16 = jnp.bfloat16
VMEM = 24 * 1024 * 1024


def lane_iota(rows, lanes=LANES):
    return lax.broadcasted_iota(jnp.int32, (rows, lanes), 1)


def row_iota(rows, lanes=LANES):
    return lax.broadcasted_iota(jnp.int32, (rows, lanes), 0)


def roll_lanes(value, shift):
    shift = shift % LANES
    return value if shift == 0 else pltpu.roll(value, shift, value.ndim - 1)


def pieces_of(value, count):
    pieces = []
    for at in range(count):
        piece = value.astype(BF16)
        pieces.append(piece)
        if at < count - 1:
            value = value - piece.astype(F32)
    return pieces


def pack_kernel(peers, fields_ref, out_ref, first_ref, last_ref, own):
    _, extent_x, extent_z, extent_y = fields_ref.shape
    half = extent_x // 2
    group = FIELDS * extent_z
    for x_at in range(extent_x):
        for field in range(FIELDS):
            base = (x_at % half) * group + field * extent_z
            rows = slice(base, base + extent_z)
            own[x_at // half, rows, :] = fields_ref[field, x_at]
    blank = jnp.zeros((LANES - half * group, LANES), F32)
    gap = jnp.zeros((HALO, LANES), F32)
    width = extent_y // peers
    for part in range(2):
        turned = []
        for tile in range(extent_y // LANES):
            value = own[part, : half * group, tile * LANES : (tile + 1) * LANES]
            turned.append(jnp.concatenate([value, blank], axis=0).T)
        whole = jnp.concatenate([gap] + turned + [gap], axis=0)
        for peer in range(peers):
            out_ref[peer, part] = whole[peer * width : peer * width + width + 2 * HALO]
        first_ref[part] = whole[HALO : 2 * HALO]
        last_ref[part] = whole[extent_y : extent_y + HALO]


def matrix_kernel(peers, extent_z, rows_ref, spread, matrix):
    size_z = peers * extent_z
    used = VARS * size_z
    group = FIELDS * extent_z

    row, lane = row_iota(LANES, 2 * LANES), lane_iota(LANES, 2 * LANES)
    column = lane % LANES
    wanted = jnp.where(lane < LANES, column // size_z, VARS)
    source_z = (row // group) * extent_z + row % extent_z
    hit = ((row % group) // extent_z == wanted) & (source_z == column % size_z)
    hit = hit & (column < used) & (row < peers * group)
    pick = jnp.where(hit, 1.0, 0.0).astype(BF16)
    for at in range(3):
        spread[at * LANES : (at + 1) * LANES, :] = pick

    row_z = row_iota(size_z)
    lane_z = lane_iota(size_z)
    ahead = jnp.where(lane_z < used, row_z - lane_z % size_z, LANES)
    lanes = lane_iota(used)
    rest = used - (LANES - used)
    blocks = []
    for along_x in range(3):
        parts_y = []
        for along_y in range(3):
            groups = []
            for source in range(VARS):
                total = jnp.zeros((size_z, LANES), F32)
                for along_z in range(3):
                    line = (9 * along_x + 3 * along_z + along_y) * VARS + source
                    total = jnp.where(ahead == along_z - 1, rows_ref[line : line + 1, :], total)
                groups.append(total)
            parts_y.append(jnp.concatenate(groups, axis=0))
        first = jnp.where(lanes < used, parts_y[1], roll_lanes(parts_y[2], used))
        second = jnp.where(lanes < used, parts_y[0], roll_lanes(parts_y[2], 2 * used))
        second = jnp.where(lanes < used + used - (LANES - used), second, 0.0)
        blocks.append(jnp.concatenate([first, second], axis=1))
    blocks.append(jnp.zeros((2 * LANES - 3 * used, 2 * LANES), F32))
    high, low = pieces_of(jnp.concatenate(blocks, axis=0), 2)
    matrix[: 2 * LANES, :] = high
    matrix[2 * LANES : 4 * LANES, :] = high
    matrix[4 * LANES :, :] = low


def powers_kernel(
    own_x, extent_z, before_ref, here_ref, after_ref, spread, matrix, basis_ref, gram_ref, even, odd, cond
):
    peers, parts, wide_y, _ = here_ref.shape
    size_z = peers * extent_z
    used = VARS * size_z
    group = FIELDS * extent_z
    half = own_x // parts
    wide_x = 3 * parts * half
    own_y = wide_y - 2 * HALO

    at_x, at_y, at_z = (lax.axis_index(axis) for axis in ("gx", "gy", "gz"))
    count_x, count_y = lax.axis_size("gx"), lax.axis_size("gy")
    column_y = row_iota(wide_y) + ((at_y * peers + at_z) * own_y - HALO)
    inside_y = (column_y >= 0) & (column_y < count_y * peers * own_y)
    lane = lane_iota(wide_y)
    for block, ref in enumerate((before_ref, here_ref, after_ref)):
        block_x = at_x + (block - 1)
        inside = inside_y & (block_x >= 0) & (block_x < count_x)
        for part in range(parts):
            tiles = [ref[peer, part] for peer in range(peers)]
            gathered = []
            for x_local in range(half):
                total = roll_lanes(tiles[0], -x_local * group)
                for peer in range(1, peers):
                    moved = roll_lanes(tiles[peer], (peer - x_local) * group)
                    total = jnp.where(lane < peer * group, total, moved)
                gathered.append(total)
            split = pieces_of(jnp.concatenate(gathered, axis=0), 3)
            result = jnp.dot(jnp.concatenate(split, axis=1), spread[...], preferred_element_type=F32)
            for x_local in range(half):
                x_at = (block * parts + part) * half + x_local
                rows = slice(x_local * wide_y, (x_local + 1) * wide_y)
                field = result[rows, :LANES]
                weight = jnp.where(inside, result[rows, LANES:], 0.0)
                cond[x_at] = weight
                even[x_at + 1] = weight * field
                if block == 1:
                    basis_ref[0, part * half + x_local] = field[HALO : HALO + own_y]

    def apply(power, now, later, x_from, count):
        near = [now[x_from + at] for at in range(count + 2)]
        firsts, seconds = [], []
        for at in range(count):
            middle = roll_lanes(near[at + 1], used)
            firsts.append(jnp.where(lane < used, near[at], middle))
            last = roll_lanes(near[at + 2], 2 * used)
            seconds.append(jnp.where(lane < 2 * used - LANES, middle, last))
        stacked = jnp.concatenate(
            [jnp.concatenate(firsts, axis=0), jnp.concatenate(seconds, axis=0)], axis=1
        )
        high, low = pieces_of(stacked, 2)
        product = jnp.dot(jnp.concatenate([high, low, high], axis=1), matrix[...], preferred_element_type=F32)
        for at in range(count):
            x_at = x_from + at
            left = product[at * wide_y : (at + 1) * wide_y, :LANES]
            right = product[at * wide_y : (at + 1) * wide_y, LANES:]
            ahead = jnp.where(lane < LANES - used, roll_lanes(left, -used), roll_lanes(right, -2 * used))
            total = left + pltpu.roll(right, 1, 0) + pltpu.roll(ahead, wide_y - 1, 0)
            weight = cond[x_at]
            value = weight * total
            if 0 <= x_at - own_x < own_x:
                basis_ref[power, x_at - own_x] = value[HALO : HALO + own_y]
            if power < POWERS:
                later[x_at + 1] = weight * value

    slots = (even, odd)
    for power in range(1, POWERS + 1):
        for x_from, x_to in spans(power, wide_x - power):
            apply(power, slots[(power + 1) % 2], slots[power % 2], x_from, x_to - x_from)

    def add(x_at, sums):
        for tile in range(own_y // 8):
            tiles = [basis_ref[power, x_at, tile * 8 : (tile + 1) * 8, :] for power in range(POWERS + 1)]
            sums = tuple(total + tiles[i] * tiles[j] for total, (i, j) in zip(sums, PAIRS))
        return sums

    sums = lax.fori_loop(0, own_x, add, tuple(jnp.zeros((8, LANES), F32) for _ in PAIRS))
    lines = [jnp.sum(total, axis=0, keepdims=True) for total in sums]
    lines.append(jnp.zeros((LANES - len(PAIRS), LANES), F32))
    table = jnp.concatenate(lines, axis=0)
    line = lax.dot_general(
        jnp.ones((8, LANES), F32),
        table,
        (((1,), (1,)), ((), ())),
        precision=lax.Precision.HIGHEST,
        preferred_element_type=F32,
    )[:1]
    gram_ref[...] = line


def spans(start, stop):
    count = -(-(stop - start) // CHUNK)
    marks = [start + (stop - start) * at // count for at in range(count + 1)]
    return list(zip(marks[:-1], marks[1:]))


def solve(gram):
    paired = [[gram[i][j] + gram[i + 1][j] for j in range(STEPS + 1)] for i in range(STEPS)]
    normal = [[paired[i][j] + paired[i][j + 1] for j in range(STEPS)] for i in range(STEPS)]
    target = [paired[i][0] for i in range(STEPS)]
    lower = [[None] * STEPS for _ in range(STEPS)]
    inverse = []
    for col in range(STEPS):
        value = normal[col][col]
        for k in range(col):
            value = value - lower[col][k] * lower[col][k]
        root = jnp.sqrt(value)
        lower[col][col] = root
        inverse.append(1.0 / root)
        for row in range(col + 1, STEPS):
            value = normal[row][col]
            for k in range(col):
                value = value - lower[row][k] * lower[col][k]
            lower[row][col] = value * inverse[col]
    forward = []
    for row in range(STEPS):
        value = target[row]
        for col in range(row):
            value = value - lower[row][col] * forward[col]
        forward.append(value * inverse[row])
    coefs = [None] * STEPS
    for row in range(STEPS - 1, -1, -1):
        value = forward[row]
        for col in range(row + 1, STEPS):
            value = value - lower[col][row] * coefs[col]
        coefs[row] = value * inverse[row]
    return coefs


def remainder(coefs):
    inner = [-(coefs[k - 1] + coefs[k]) for k in range(1, STEPS)]
    return [1.0 - coefs[0]] + inner + [-coefs[STEPS - 1]]


def turn_kernel(peers, basis_ref, out_ref, turned):
    _, own_x, _, _ = basis_ref.shape
    extent_z = out_ref.shape[2] // (own_x * VARS)
    for pair in range(POWERS // 2):
        for x_at in range(own_x):
            both = jnp.concatenate([basis_ref[2 * pair + 1, x_at], basis_ref[2 * pair + 2, x_at]], axis=0)
            turned[pair, x_at] = both.T
            for peer in range(peers):
                for var in range(VARS):
                    source = (var * peers + peer) * extent_z
                    place = (x_at * VARS + var) * extent_z
                    out_ref[peer, pair, place : place + extent_z, :] = turned[
                        pair, x_at, source : source + extent_z, :
                    ]


def finish_kernel(grams_ref, first_ref, *refs):
    parts, (solution_ref, residual_ref, solutions, residuals) = refs[:-4], refs[-4:]
    peers = len(parts)
    _, extent_x, extent_z, extent_y = first_ref.shape
    line = jnp.sum(grams_ref[...], axis=0)
    where = lane_iota(1)
    entry = {}
    for at, (i, j) in enumerate(PAIRS):
        value = jnp.sum(jnp.where(where == at, line, 0.0), axis=1, keepdims=True)
        entry[i, j] = entry[j, i] = value
    first = solve([[entry[i, j] for j in range(STEPS + 1)] for i in range(STEPS + 1)])
    left = remainder(first)
    half = {}
    for i in range(STEPS + 1):
        for j in range(POWERS + 1):
            value = left[0] * entry[i, j]
            for k in range(1, STEPS + 1):
                value = value + left[k] * entry[i + k, j]
            half[i, j] = value
    second_gram = []
    for i in range(STEPS + 1):
        line = []
        for j in range(STEPS + 1):
            value = left[0] * half[i, j]
            for k in range(1, STEPS + 1):
                value = value + left[k] * half[i, j + k]
            line.append(value)
        second_gram.append(line)
    second = solve(second_gram)
    last = remainder(second)
    of_solution = list(first) + [0.0] * STEPS
    of_residual = [0.0] * (POWERS + 1)
    for i in range(STEPS):
        for k in range(STEPS + 1):
            of_solution[i + k] = of_solution[i + k] + second[i] * left[k]
    for i in range(STEPS + 1):
        for k in range(STEPS + 1):
            of_residual[i + k] = of_residual[i + k] + last[i] * left[k]
    of_solution.append(0.0)
    middle = LANES // 2
    pick = lane_iota(1) < middle

    def paired(coefs, pair):
        return jnp.where(pick, coefs[2 * pair + 1], coefs[2 * pair + 2])

    at_z = lax.axis_index("gz")
    for shift, ref in enumerate(parts):
        chunk = lax.rem(at_z + peers - shift, peers)
        for coefs, sums in ((of_solution, solutions), (of_residual, residuals)):
            total = paired(coefs, 0) * ref[0]
            for pair in range(1, POWERS // 2):
                total = total + paired(coefs, pair) * ref[pair]
            sums[chunk] = total + roll_lanes(total, middle)
    lanes = lane_iota(extent_z)
    for x_at in range(extent_x):
        for var in range(VARS):
            place = (x_at * VARS + var) * extent_z
            rows = slice(place, place + extent_z)
            for tile in range(extent_y // LANES):
                columns = slice(tile * LANES, (tile + 1) * LANES)
                first_part = first_ref[var, x_at, :, columns]
                for coefs, sums, ref in (
                    (of_solution, solutions, solution_ref),
                    (of_residual, residuals, residual_ref),
                ):
                    rest = jnp.where(lanes < middle, sums[2 * tile, rows, :], sums[2 * tile + 1, rows, :])
                    ref[var, x_at, :, columns] = coefs[0] * first_part + rest


def call(kernel, out_shape, scratch=(), **more):
    return pl.pallas_call(
        kernel,
        out_shape=out_shape,
        scratch_shapes=scratch,
        compiler_params=pltpu.CompilerParams(vmem_limit_bytes=VMEM),
        **more,
    )


def ring(count):
    up = [(i, (i + 1) % count) for i in range(count)]
    return up, [(j, i) for i, j in up]


def per_device(right_side, conductance, blocks):
    count_x, count_y, count_z = (lax.axis_size(axis) for axis in ("gx", "gy", "gz"))
    _, extent_x, extent_z, extent_y = right_side.shape
    size_z = extent_z * count_z
    own_y = extent_y // count_z
    wide_y = own_y + 2 * HALO

    edge = jax.ShapeDtypeStruct((2, HALO, LANES), F32)
    strips, first, last = call(
        functools.partial(pack_kernel, count_z),
        (jax.ShapeDtypeStruct((count_z, 2, wide_y, LANES), F32), edge, edge),
        (pltpu.VMEM((2, LANES, extent_y), F32),),
    )(jnp.concatenate([right_side, conductance[None]], axis=0))
    up, down = ring(count_y)
    left = lax.ppermute(last, "gy", up)
    right = lax.ppermute(first, "gy", down)
    strips = strips.at[0, :, :HALO].set(left).at[count_z - 1, :, wide_y - HALO :].set(right)
    here = lax.all_to_all(strips, "gz", 0, 0, tiled=True)
    up, down = ring(count_x)
    before = lax.ppermute(here, "gx", up)
    after = lax.ppermute(here, "gx", down)

    rows = jnp.repeat(blocks.transpose(0, 2, 1).reshape(-1, VARS), size_z, axis=1)
    rows = jnp.pad(rows, ((0, 1), (0, LANES - VARS * size_z)))
    spread, matrix = call(
        functools.partial(matrix_kernel, count_z, extent_z),
        (
            jax.ShapeDtypeStruct((3 * LANES, 2 * LANES), BF16),
            jax.ShapeDtypeStruct((6 * LANES, 2 * LANES), BF16),
        ),
    )(rows)
    basis, gram = call(
        functools.partial(powers_kernel, extent_x, extent_z),
        (
            jax.ShapeDtypeStruct((POWERS + 1, extent_x, own_y, LANES), F32),
            jax.ShapeDtypeStruct((1, LANES), F32),
        ),
        (
            pltpu.VMEM((3 * extent_x + 2, wide_y, LANES), F32),
            pltpu.VMEM((3 * extent_x + 2, wide_y, LANES), F32),
            pltpu.VMEM((3 * extent_x, wide_y, LANES), F32),
        ),
    )(before, here, after, spread, matrix)

    pairs = [(i, i ^ 1) for i in range(count_y)]
    gram = gram + lax.ppermute(gram, "gy", pairs)
    chips = count_x * count_y * count_z // 2
    groups = [
        [(x * count_y + y) * count_z + z for x in range(count_x) for y in range(core, count_y, 2) for z in range(count_z)]
        for core in range(2)
    ]
    grams = jnp.broadcast_to(gram[None], (chips, 1, LANES))
    grams = lax.all_to_all(grams, ("gx", "gy", "gz"), 0, 0, tiled=True, axis_index_groups=groups)

    turned = call(
        functools.partial(turn_kernel, count_z),
        jax.ShapeDtypeStruct((count_z, POWERS // 2, extent_x * VARS * extent_z, LANES), F32),
        (pltpu.VMEM((POWERS // 2, extent_x, LANES, LANES), F32),),
    )(basis)
    at_z = lax.axis_index("gz")
    parts = []
    for shift in range(count_z):
        part = lax.dynamic_index_in_dim(turned, (at_z + shift) % count_z, 0, keepdims=False)
        if shift > 0:
            part = lax.ppermute(part, "gz", [(i, (i + shift) % count_z) for i in range(count_z)])
        parts.append(part)
    shape = jax.ShapeDtypeStruct(right_side.shape, F32)
    scratch = pltpu.VMEM((count_z, extent_x * VARS * extent_z, LANES), F32)
    return call(finish_kernel, (shape, shape), (scratch, scratch))(grams, right_side, *parts)


def solution(mesh):
    in_specs = (P(None, "gx", "gz", "gy"), P("gx", "gz", "gy"), P())
    out_specs = (P(None, "gx", "gz", "gy"), P(None, "gx", "gz", "gy"))
    return jax.shard_map(
        per_device, mesh=mesh, in_specs=in_specs, out_specs=out_specs, check_vma=False
    )
```

```python
import functools

import jax
import jax.numpy as jnp
from jax import lax
from jax.experimental import pallas as pl
from jax.experimental.pallas import tpu as pltpu
from jax.sharding import PartitionSpec as P

STEPS = 4
POWERS = 2 * STEPS
VARS = 5
FIELDS = VARS + 1
HALO = POWERS
LANES = 128
CHUNK = 10
PAIRS = [(i, j) for i in range(POWERS + 1) for j in range(i, POWERS + 1)]

F32 = jnp.float32
BF16 = jnp.bfloat16
VMEM = 24 * 1024 * 1024


def lane_iota(rows, lanes=LANES):
    return lax.broadcasted_iota(jnp.int32, (rows, lanes), 1)


def row_iota(rows, lanes=LANES):
    return lax.broadcasted_iota(jnp.int32, (rows, lanes), 0)


def roll_lanes(value, shift):
    shift = shift % LANES
    return value if shift == 0 else pltpu.roll(value, shift, value.ndim - 1)


def pieces_of(value, count):
    pieces = []
    for at in range(count):
        piece = value.astype(BF16)
        pieces.append(piece)
        if at < count - 1:
            value = value - piece.astype(F32)
    return pieces


def pack_kernel(peers, fields_ref, out_ref, first_ref, last_ref, own):
    _, extent_x, extent_z, extent_y = fields_ref.shape
    group = FIELDS * extent_z
    for x_at in range(extent_x):
        for field in range(FIELDS):
            base = x_at * group + field * extent_z
            own[base : base + extent_z, :] = fields_ref[field, x_at]
    rest = extent_x * group - LANES
    own[LANES + rest :, :] = jnp.zeros((LANES - rest, extent_y), F32)
    gap = jnp.zeros((HALO, LANES), F32)
    width = extent_y // peers
    wide = width + 2 * HALO
    halves = lane_iota(wide // 2) < LANES // 2
    for part in range(2):
        turned = []
        for tile in range(extent_y // LANES):
            turned.append(own[part * LANES : (part + 1) * LANES, tile * LANES : (tile + 1) * LANES].T)
        whole = jnp.concatenate([gap] + turned + [gap], axis=0)
        for peer in range(peers):
            strip = whole[peer * width : peer * width + wide]
            if part == 0:
                out_ref[peer, :wide] = strip
            else:
                beside = roll_lanes(strip[wide // 2 :], LANES // 2)
                out_ref[peer, wide:] = jnp.where(halves, strip[: wide // 2], beside)
        for ref, start in ((first_ref, HALO), (last_ref, extent_y)):
            value = whole[start : start + HALO]
            if part == 1:
                value = jnp.where(halves[:HALO], value, roll_lanes(value, LANES // 2))
            ref[part] = value


def edge_kernel(wide, strips_ref, left_ref, right_ref, out_ref):
    peers, rows, _ = strips_ref.shape
    lower = lane_iota(HALO) < LANES // 2
    out_ref[...] = strips_ref[...]
    out_ref[0, :HALO] = left_ref[0]
    out_ref[0, wide : wide + HALO] = jnp.where(lower, left_ref[1], strips_ref[0, wide : wide + HALO])
    out_ref[peers - 1, wide - HALO : wide] = right_ref[0]
    out_ref[peers - 1, rows - HALO :] = jnp.where(lower, strips_ref[peers - 1, rows - HALO :], right_ref[1])


def matrix_kernel(peers, extent_z, rows_ref, spread, matrix):
    size_z = peers * extent_z
    used = VARS * size_z
    group = FIELDS * extent_z

    row, lane = row_iota(LANES, 2 * LANES), lane_iota(LANES, 2 * LANES)
    column = lane % LANES
    wanted = jnp.where(lane < LANES, column // size_z, VARS)
    source_z = (row // group) * extent_z + row % extent_z
    hit = ((row % group) // extent_z == wanted) & (source_z == column % size_z)
    hit = hit & (column < used) & (row < peers * group)
    pick = jnp.where(hit, 1.0, 0.0).astype(BF16)
    for at in range(3):
        spread[at * LANES : (at + 1) * LANES, :] = pick

    row_z = row_iota(size_z)
    lane_z = lane_iota(size_z)
    ahead = jnp.where(lane_z < used, row_z - lane_z % size_z, LANES)
    lanes = lane_iota(used)
    rest = used - (LANES - used)
    blocks = []
    for along_x in range(3):
        parts_y = []
        for along_y in range(3):
            groups = []
            for source in range(VARS):
                total = jnp.zeros((size_z, LANES), F32)
                for along_z in range(3):
                    line = (9 * along_x + 3 * along_z + along_y) * VARS + source
                    total = jnp.where(ahead == along_z - 1, rows_ref[line : line + 1, :], total)
                groups.append(total)
            parts_y.append(jnp.concatenate(groups, axis=0))
        first = jnp.where(lanes < used, parts_y[1], roll_lanes(parts_y[2], used))
        second = jnp.where(lanes < used, parts_y[0], roll_lanes(parts_y[2], 2 * used))
        second = jnp.where(lanes < used + used - (LANES - used), second, 0.0)
        blocks.append(jnp.concatenate([first, second], axis=1))
    blocks.append(jnp.zeros((2 * LANES - 3 * used, 2 * LANES), F32))
    high, low = pieces_of(jnp.concatenate(blocks, axis=0), 2)
    matrix[: 2 * LANES, :] = high
    matrix[2 * LANES : 4 * LANES, :] = high
    matrix[4 * LANES :, :] = low


def powers_kernel(
    own_x, extent_z, before_ref, here_ref, after_ref, spread, matrix, basis_ref, gram_ref, even, odd, cond
):
    peers = here_ref.shape[0]
    wide_y = cond.shape[1]
    size_z = peers * extent_z
    used = VARS * size_z
    group = FIELDS * extent_z
    half = own_x // 2
    wide_x = 3 * own_x
    own_y = wide_y - 2 * HALO

    at_x, at_y, at_z = (lax.axis_index(axis) for axis in ("gx", "gy", "gz"))
    count_x, count_y = lax.axis_size("gx"), lax.axis_size("gy")
    column_y = row_iota(wide_y) + ((at_y * peers + at_z) * own_y - HALO)
    inside_y = (column_y >= 0) & (column_y < count_y * peers * own_y)
    lane = lane_iota(wide_y)
    for block, ref in enumerate((before_ref, here_ref, after_ref)):
        block_x = at_x + (block - 1)
        inside = inside_y & (block_x >= 0) & (block_x < count_x)
        whole, rest = [], []
        for peer in range(peers):
            whole.append(ref[peer, :wide_y])
            packed = ref[peer, wide_y:]
            rest.append(jnp.concatenate([packed, roll_lanes(packed, LANES // 2)], axis=0))

        def moved(peer, start):
            place = peer * group
            if start >= LANES:
                return roll_lanes(rest[peer], place - (start - LANES))
            value = roll_lanes(whole[peer], place - start)
            if start + group > LANES:
                edge = place + LANES - start
                value = jnp.where(lane < edge, value, roll_lanes(rest[peer], edge))
            return value

        for part in range(2):
            gathered = []
            for x_local in range(half):
                start = (part * half + x_local) * group
                total = moved(0, start)
                for peer in range(1, peers):
                    total = jnp.where(lane < peer * group, total, moved(peer, start))
                gathered.append(total)
            split = pieces_of(jnp.concatenate(gathered, axis=0), 3)
            result = jnp.dot(jnp.concatenate(split, axis=1), spread[...], preferred_element_type=F32)
            for x_local in range(half):
                x_at = (block * 2 + part) * half + x_local
                rows = slice(x_local * wide_y, (x_local + 1) * wide_y)
                field = result[rows, :LANES]
                weight = jnp.where(inside, result[rows, LANES:], 0.0)
                cond[x_at] = weight
                even[x_at + 1] = weight * field
                if block == 1:
                    basis_ref[0, part * half + x_local] = field[HALO : HALO + own_y]

    def apply(power, now, later, x_from, count):
        near = [now[x_from + at] for at in range(count + 2)]
        firsts, seconds = [], []
        for at in range(count):
            middle = roll_lanes(near[at + 1], used)
            firsts.append(jnp.where(lane < used, near[at], middle))
            last = roll_lanes(near[at + 2], 2 * used)
            seconds.append(jnp.where(lane < 2 * used - LANES, middle, last))
        stacked = jnp.concatenate(
            [jnp.concatenate(firsts, axis=0), jnp.concatenate(seconds, axis=0)], axis=1
        )
        high, low = pieces_of(stacked, 2)
        product = jnp.dot(jnp.concatenate([high, low, high], axis=1), matrix[...], preferred_element_type=F32)
        for at in range(count):
            x_at = x_from + at
            left = product[at * wide_y : (at + 1) * wide_y, :LANES]
            right = product[at * wide_y : (at + 1) * wide_y, LANES:]
            ahead = jnp.where(lane < LANES - used, roll_lanes(left, -used), roll_lanes(right, -2 * used))
            total = left + pltpu.roll(right, 1, 0) + pltpu.roll(ahead, wide_y - 1, 0)
            weight = cond[x_at]
            value = weight * total
            if 0 <= x_at - own_x < own_x:
                basis_ref[power, x_at - own_x] = value[HALO : HALO + own_y]
            if power < POWERS:
                later[x_at + 1] = weight * value

    slots = (even, odd)
    for power in range(1, POWERS + 1):
        for x_from, x_to in spans(power, wide_x - power):
            apply(power, slots[(power + 1) % 2], slots[power % 2], x_from, x_to - x_from)

    def add(x_at, sums):
        for tile in range(own_y // 8):
            tiles = [basis_ref[power, x_at, tile * 8 : (tile + 1) * 8, :] for power in range(POWERS + 1)]
            sums = tuple(total + tiles[i] * tiles[j] for total, (i, j) in zip(sums, PAIRS))
        return sums

    sums = lax.fori_loop(0, own_x, add, tuple(jnp.zeros((8, LANES), F32) for _ in PAIRS))
    lines = [jnp.sum(total, axis=0, keepdims=True) for total in sums]
    lines.append(jnp.zeros((LANES - len(PAIRS), LANES), F32))
    table = jnp.concatenate(lines, axis=0)
    line = lax.dot_general(
        jnp.ones((8, LANES), F32),
        table,
        (((1,), (1,)), ((), ())),
        precision=lax.Precision.HIGHEST,
        preferred_element_type=F32,
    )[:1]
    gram_ref[...] = line


def spans(start, stop):
    count = -(-(stop - start) // CHUNK)
    marks = [start + (stop - start) * at // count for at in range(count + 1)]
    return list(zip(marks[:-1], marks[1:]))


def solve(gram):
    paired = [[gram[i][j] + gram[i + 1][j] for j in range(STEPS + 1)] for i in range(STEPS)]
    normal = [[paired[i][j] + paired[i][j + 1] for j in range(STEPS)] for i in range(STEPS)]
    target = [paired[i][0] for i in range(STEPS)]
    lower = [[None] * STEPS for _ in range(STEPS)]
    inverse = []
    for col in range(STEPS):
        value = normal[col][col]
        for k in range(col):
            value = value - lower[col][k] * lower[col][k]
        root = jnp.sqrt(value)
        lower[col][col] = root
        inverse.append(1.0 / root)
        for row in range(col + 1, STEPS):
            value = normal[row][col]
            for k in range(col):
                value = value - lower[row][k] * lower[col][k]
            lower[row][col] = value * inverse[col]
    forward = []
    for row in range(STEPS):
        value = target[row]
        for col in range(row):
            value = value - lower[row][col] * forward[col]
        forward.append(value * inverse[row])
    coefs = [None] * STEPS
    for row in range(STEPS - 1, -1, -1):
        value = forward[row]
        for col in range(row + 1, STEPS):
            value = value - lower[col][row] * coefs[col]
        coefs[row] = value * inverse[row]
    return coefs


def remainder(coefs):
    inner = [-(coefs[k - 1] + coefs[k]) for k in range(1, STEPS)]
    return [1.0 - coefs[0]] + inner + [-coefs[STEPS - 1]]


def turn_kernel(peers, basis_ref, out_ref, turned):
    _, own_x, _, _ = basis_ref.shape
    extent_z = out_ref.shape[2] // (own_x * VARS)
    for pair in range(POWERS // 2):
        for x_at in range(own_x):
            both = jnp.concatenate([basis_ref[2 * pair + 1, x_at], basis_ref[2 * pair + 2, x_at]], axis=0)
            turned[pair, x_at] = both.T
            for peer in range(peers):
                for var in range(VARS):
                    source = (var * peers + peer) * extent_z
                    place = (x_at * VARS + var) * extent_z
                    out_ref[peer, pair, place : place + extent_z, :] = turned[
                        pair, x_at, source : source + extent_z, :
                    ]


def finish_kernel(grams_ref, first_ref, *refs):
    parts, (solution_ref, residual_ref, solutions, residuals) = refs[:-4], refs[-4:]
    peers = len(parts)
    _, extent_x, extent_z, extent_y = first_ref.shape
    line = jnp.sum(grams_ref[...], axis=0)
    where = lane_iota(1)
    entry = {}
    for at, (i, j) in enumerate(PAIRS):
        value = jnp.sum(jnp.where(where == at, line, 0.0), axis=1, keepdims=True)
        entry[i, j] = entry[j, i] = value
    first = solve([[entry[i, j] for j in range(STEPS + 1)] for i in range(STEPS + 1)])
    left = remainder(first)
    half = {}
    for i in range(STEPS + 1):
        for j in range(POWERS + 1):
            value = left[0] * entry[i, j]
            for k in range(1, STEPS + 1):
                value = value + left[k] * entry[i + k, j]
            half[i, j] = value
    second_gram = []
    for i in range(STEPS + 1):
        line = []
        for j in range(STEPS + 1):
            value = left[0] * half[i, j]
            for k in range(1, STEPS + 1):
                value = value + left[k] * half[i, j + k]
            line.append(value)
        second_gram.append(line)
    second = solve(second_gram)
    last = remainder(second)
    of_solution = list(first) + [0.0] * STEPS
    of_residual = [0.0] * (POWERS + 1)
    for i in range(STEPS):
        for k in range(STEPS + 1):
            of_solution[i + k] = of_solution[i + k] + second[i] * left[k]
    for i in range(STEPS + 1):
        for k in range(STEPS + 1):
            of_residual[i + k] = of_residual[i + k] + last[i] * left[k]
    of_solution.append(0.0)
    middle = LANES // 2
    pick = lane_iota(1) < middle

    def paired(coefs, pair):
        return jnp.where(pick, coefs[2 * pair + 1], coefs[2 * pair + 2])

    at_z = lax.axis_index("gz")
    for shift, ref in enumerate(parts):
        chunk = lax.rem(at_z + peers - shift, peers)
        for coefs, sums in ((of_solution, solutions), (of_residual, residuals)):
            total = paired(coefs, 0) * ref[0]
            for pair in range(1, POWERS // 2):
                total = total + paired(coefs, pair) * ref[pair]
            sums[chunk] = total + roll_lanes(total, middle)
    lanes = lane_iota(extent_z)
    for x_at in range(extent_x):
        for var in range(VARS):
            place = (x_at * VARS + var) * extent_z
            rows = slice(place, place + extent_z)
            for tile in range(extent_y // LANES):
                columns = slice(tile * LANES, (tile + 1) * LANES)
                first_part = first_ref[var, x_at, :, columns]
                for coefs, sums, ref in (
                    (of_solution, solutions, solution_ref),
                    (of_residual, residuals, residual_ref),
                ):
                    rest = jnp.where(lanes < middle, sums[2 * tile, rows, :], sums[2 * tile + 1, rows, :])
                    ref[var, x_at, :, columns] = coefs[0] * first_part + rest


def call(kernel, out_shape, scratch=(), **more):
    return pl.pallas_call(
        kernel,
        out_shape=out_shape,
        scratch_shapes=scratch,
        compiler_params=pltpu.CompilerParams(vmem_limit_bytes=VMEM),
        **more,
    )


def ring(count):
    up = [(i, (i + 1) % count) for i in range(count)]
    return up, [(j, i) for i, j in up]


def per_device(right_side, conductance, blocks):
    count_x, count_y, count_z = (lax.axis_size(axis) for axis in ("gx", "gy", "gz"))
    _, extent_x, extent_z, extent_y = right_side.shape
    size_z = extent_z * count_z
    own_y = extent_y // count_z
    wide_y = own_y + 2 * HALO

    edge = jax.ShapeDtypeStruct((2, HALO, LANES), F32)
    strips, first, last = call(
        functools.partial(pack_kernel, count_z),
        (jax.ShapeDtypeStruct((count_z, wide_y + wide_y // 2, LANES), F32), edge, edge),
        (pltpu.VMEM((2 * LANES, extent_y), F32),),
    )(jnp.concatenate([right_side, conductance[None]], axis=0))
    up, down = ring(count_y)
    left = lax.ppermute(last, "gy", up)
    right = lax.ppermute(first, "gy", down)
    strips = call(
        functools.partial(edge_kernel, wide_y), jax.ShapeDtypeStruct(strips.shape, F32)
    )(strips, left, right)
    here = lax.all_to_all(strips, "gz", 0, 0, tiled=True)
    up, down = ring(count_x)
    before = lax.ppermute(here, "gx", up)
    after = lax.ppermute(here, "gx", down)

    rows = jnp.repeat(blocks.transpose(0, 2, 1).reshape(-1, VARS), size_z, axis=1)
    rows = jnp.pad(rows, ((0, 1), (0, LANES - VARS * size_z)))
    spread, matrix = call(
        functools.partial(matrix_kernel, count_z, extent_z),
        (
            jax.ShapeDtypeStruct((3 * LANES, 2 * LANES), BF16),
            jax.ShapeDtypeStruct((6 * LANES, 2 * LANES), BF16),
        ),
    )(rows)
    basis, gram = call(
        functools.partial(powers_kernel, extent_x, extent_z),
        (
            jax.ShapeDtypeStruct((POWERS + 1, extent_x, own_y, LANES), F32),
            jax.ShapeDtypeStruct((1, LANES), F32),
        ),
        (
            pltpu.VMEM((3 * extent_x + 2, wide_y, LANES), F32),
            pltpu.VMEM((3 * extent_x + 2, wide_y, LANES), F32),
            pltpu.VMEM((3 * extent_x, wide_y, LANES), F32),
        ),
    )(before, here, after, spread, matrix)

    pairs = [(i, i ^ 1) for i in range(count_y)]
    gram = gram + lax.ppermute(gram, "gy", pairs)
    chips = count_x * count_y * count_z // 2
    groups = [
        [(x * count_y + y) * count_z + z for x in range(count_x) for y in range(core, count_y, 2) for z in range(count_z)]
        for core in range(2)
    ]
    grams = jnp.broadcast_to(gram[None], (chips, 1, LANES))
    grams = lax.all_to_all(grams, ("gx", "gy", "gz"), 0, 0, tiled=True, axis_index_groups=groups)

    turned = call(
        functools.partial(turn_kernel, count_z),
        jax.ShapeDtypeStruct((count_z, POWERS // 2, extent_x * VARS * extent_z, LANES), F32),
        (pltpu.VMEM((POWERS // 2, extent_x, LANES, LANES), F32),),
    )(basis)
    at_z = lax.axis_index("gz")
    parts = []
    for shift in range(count_z):
        part = lax.dynamic_index_in_dim(turned, (at_z + shift) % count_z, 0, keepdims=False)
        if shift > 0:
            part = lax.ppermute(part, "gz", [(i, (i + shift) % count_z) for i in range(count_z)])
        parts.append(part)
    shape = jax.ShapeDtypeStruct(right_side.shape, F32)
    scratch = pltpu.VMEM((count_z, extent_x * VARS * extent_z, LANES), F32)
    return call(finish_kernel, (shape, shape), (scratch, scratch))(grams, right_side, *parts)


def solution(mesh):
    in_specs = (P(None, "gx", "gz", "gy"), P("gx", "gz", "gy"), P())
    out_specs = (P(None, "gx", "gz", "gy"), P(None, "gx", "gz", "gy"))
    return jax.shard_map(
        per_device, mesh=mesh, in_specs=in_specs, out_specs=out_specs, check_vma=False
    )
```

```python
import functools

import jax
import jax.numpy as jnp
from jax import lax
from jax.experimental import pallas as pl
from jax.experimental.pallas import tpu as pltpu
from jax.sharding import PartitionSpec as P

STEPS = 4
POWERS = 2 * STEPS
VARS = 5
FIELDS = VARS + 1
HALO = POWERS
LANES = 128
CHUNK = 10
PAIRS = [(i, j) for i in range(POWERS + 1) for j in range(i, POWERS + 1)]

F32 = jnp.float32
BF16 = jnp.bfloat16
VMEM = 24 * 1024 * 1024


def lane_iota(rows, lanes=LANES):
    return lax.broadcasted_iota(jnp.int32, (rows, lanes), 1)


def row_iota(rows, lanes=LANES):
    return lax.broadcasted_iota(jnp.int32, (rows, lanes), 0)


def roll_lanes(value, shift):
    shift = shift % LANES
    return value if shift == 0 else pltpu.roll(value, shift, value.ndim - 1)


def pieces_of(value, count):
    pieces = []
    for at in range(count):
        piece = value.astype(BF16)
        pieces.append(piece)
        if at < count - 1:
            value = value - piece.astype(F32)
    return pieces


def pack_kernel(peers, fields_ref, out_ref, first_ref, last_ref, own):
    _, extent_x, extent_z, extent_y = fields_ref.shape
    group = FIELDS * extent_z
    for x_at in range(extent_x):
        for field in range(FIELDS):
            base = x_at * group + field * extent_z
            own[base : base + extent_z, :] = fields_ref[field, x_at]
    rest = extent_x * group - LANES
    own[LANES + rest :, :] = jnp.zeros((LANES - rest, extent_y), F32)
    gap = jnp.zeros((HALO, LANES), F32)
    width = extent_y // peers
    wide = width + 2 * HALO
    halves = lane_iota(wide // 2) < LANES // 2
    for part in range(2):
        turned = []
        for tile in range(extent_y // LANES):
            turned.append(own[part * LANES : (part + 1) * LANES, tile * LANES : (tile + 1) * LANES].T)
        whole = jnp.concatenate([gap] + turned + [gap], axis=0)
        for peer in range(peers):
            strip = whole[peer * width : peer * width + wide]
            if part == 0:
                out_ref[peer, :wide] = strip
            else:
                beside = roll_lanes(strip[wide // 2 :], LANES // 2)
                out_ref[peer, wide:] = jnp.where(halves, strip[: wide // 2], beside)
        for ref, start in ((first_ref, HALO), (last_ref, extent_y)):
            value = whole[start : start + HALO]
            if part == 1:
                value = jnp.where(halves[:HALO], value, roll_lanes(value, LANES // 2))
            ref[part] = value


def edge_kernel(wide, strips_ref, left_ref, right_ref, out_ref):
    peers, rows, _ = strips_ref.shape
    lower = lane_iota(HALO) < LANES // 2
    out_ref[...] = strips_ref[...]
    out_ref[0, :HALO] = left_ref[0]
    out_ref[0, wide : wide + HALO] = jnp.where(lower, left_ref[1], strips_ref[0, wide : wide + HALO])
    out_ref[peers - 1, wide - HALO : wide] = right_ref[0]
    out_ref[peers - 1, rows - HALO :] = jnp.where(lower, strips_ref[peers - 1, rows - HALO :], right_ref[1])


def matrix_kernel(peers, extent_z, rows_ref, spread, matrix):
    size_z = peers * extent_z
    used = VARS * size_z
    group = FIELDS * extent_z

    row, lane = row_iota(LANES, 2 * LANES), lane_iota(LANES, 2 * LANES)
    column = lane % LANES
    wanted = jnp.where(lane < LANES, column // size_z, VARS)
    source_z = (row // group) * extent_z + row % extent_z
    hit = ((row % group) // extent_z == wanted) & (source_z == column % size_z)
    hit = hit & (column < used) & (row < peers * group)
    pick = jnp.where(hit, 1.0, 0.0).astype(BF16)
    for at in range(3):
        spread[at * LANES : (at + 1) * LANES, :] = pick

    row_z = row_iota(size_z)
    lane_z = lane_iota(size_z)
    ahead = jnp.where(lane_z < used, row_z - lane_z % size_z, LANES)
    lanes = lane_iota(used)
    rest = used - (LANES - used)
    blocks = []
    for along_x in range(3):
        parts_y = []
        for along_y in range(3):
            groups = []
            for source in range(VARS):
                total = jnp.zeros((size_z, LANES), F32)
                for along_z in range(3):
                    line = (9 * along_x + 3 * along_z + along_y) * VARS + source
                    total = jnp.where(ahead == along_z - 1, rows_ref[line : line + 1, :], total)
                groups.append(total)
            parts_y.append(jnp.concatenate(groups, axis=0))
        first = jnp.where(lanes < used, parts_y[1], roll_lanes(parts_y[2], used))
        second = jnp.where(lanes < used, parts_y[0], roll_lanes(parts_y[2], 2 * used))
        second = jnp.where(lanes < used + used - (LANES - used), second, 0.0)
        blocks.append(jnp.concatenate([first, second], axis=1))
    blocks.append(jnp.zeros((2 * LANES - 3 * used, 2 * LANES), F32))
    high, low = pieces_of(jnp.concatenate(blocks, axis=0), 2)
    matrix[: 2 * LANES, :] = high
    matrix[2 * LANES : 4 * LANES, :] = high
    matrix[4 * LANES :, :] = low


def planes_of(ref, spread, own_x, extent_z, wide_y):
    peers = ref.shape[0]
    group = FIELDS * extent_z
    half = own_x // 2
    lane = lane_iota(wide_y)
    whole, rest = [], []
    for peer in range(peers):
        whole.append(ref[peer, :wide_y])
        packed = ref[peer, wide_y:]
        rest.append(jnp.concatenate([packed, roll_lanes(packed, LANES // 2)], axis=0))

    def moved(peer, start):
        place = peer * group
        if start >= LANES:
            return roll_lanes(rest[peer], place - (start - LANES))
        value = roll_lanes(whole[peer], place - start)
        if start + group > LANES:
            edge = place + LANES - start
            value = jnp.where(lane < edge, value, roll_lanes(rest[peer], edge))
        return value

    planes = []
    for part in range(2):
        gathered = []
        for x_local in range(half):
            start = (part * half + x_local) * group
            total = moved(0, start)
            for peer in range(1, peers):
                total = jnp.where(lane < peer * group, total, moved(peer, start))
            gathered.append(total)
        split = pieces_of(jnp.concatenate(gathered, axis=0), 3)
        result = jnp.dot(jnp.concatenate(split, axis=1), spread[...], preferred_element_type=F32)
        for x_local in range(half):
            rows = slice(x_local * wide_y, (x_local + 1) * wide_y)
            planes.append((result[rows, :LANES], result[rows, LANES:]))
    return planes


def within(block, peers, own_y, wide_y):
    at_x, at_y, at_z = (lax.axis_index(axis) for axis in ("gx", "gy", "gz"))
    column = row_iota(wide_y) + ((at_y * peers + at_z) * own_y - HALO)
    inside = (column >= 0) & (column < lax.axis_size("gy") * peers * own_y)
    block_x = at_x + (block - 1)
    return inside & (block_x >= 0) & (block_x < lax.axis_size("gx"))


def apply(used, wide_y, matrix, x_from, x_to, get, weight_of, put):
    lane = lane_iota(wide_y)
    near = [get(x_at) for x_at in range(x_from - 1, x_to + 1)]
    firsts, seconds = [], []
    for at in range(x_to - x_from):
        middle = roll_lanes(near[at + 1], used)
        firsts.append(jnp.where(lane < used, near[at], middle))
        last = roll_lanes(near[at + 2], 2 * used)
        seconds.append(jnp.where(lane < 2 * used - LANES, middle, last))
    stacked = jnp.concatenate([jnp.concatenate(firsts, axis=0), jnp.concatenate(seconds, axis=0)], axis=1)
    high, low = pieces_of(stacked, 2)
    product = jnp.dot(jnp.concatenate([high, low, high], axis=1), matrix[...], preferred_element_type=F32)
    for at in range(x_to - x_from):
        left = product[at * wide_y : (at + 1) * wide_y, :LANES]
        right = product[at * wide_y : (at + 1) * wide_y, LANES:]
        ahead = jnp.where(lane < LANES - used, roll_lanes(left, -used), roll_lanes(right, -2 * used))
        total = left + pltpu.roll(right, 1, 0) + pltpu.roll(ahead, wide_y - 1, 0)
        weight = weight_of(x_from + at)
        value = weight * total
        put(x_from + at, value, weight * value)


def own_kernel(own_x, extent_z, here_ref, spread, matrix, cond_ref, scaled_ref, basis_ref):
    peers = here_ref.shape[0]
    wide_y, own_y = scaled_ref.shape[2], basis_ref.shape[2]
    used = VARS * peers * extent_z
    inside = within(1, peers, own_y, wide_y)
    for at, (field, weight) in enumerate(planes_of(here_ref, spread, own_x, extent_z, wide_y)):
        weight = jnp.where(inside, weight, 0.0)
        cond_ref[at] = weight
        scaled_ref[0, at] = weight * field
        basis_ref[0, at] = field[HALO : HALO + own_y]
    for power in range(1, STEPS):

        def get(x_at, power=power):
            return scaled_ref[power - 1, x_at]

        def put(x_at, value, scaled, power=power):
            basis_ref[power, x_at] = value[HALO : HALO + own_y]
            scaled_ref[power, x_at] = scaled

        apply(used, wide_y, matrix, power, own_x - power, get, lambda x_at: cond_ref[x_at], put)


def powers_kernel(
    own_x,
    extent_z,
    before_ref,
    after_ref,
    own_cond,
    own_scaled,
    own_basis,
    spread,
    matrix,
    basis_ref,
    gram_ref,
    even,
    odd,
    cond,
):
    peers = before_ref.shape[0]
    _, wide_y, _ = cond.shape
    used = VARS * peers * extent_z
    wide_x = 3 * own_x
    own_y = wide_y - 2 * HALO
    slots = (even, odd)

    def known(power, x_at):
        return power < STEPS and own_x + power <= x_at < 2 * own_x - power

    for block, ref in ((0, before_ref), (2, after_ref)):
        inside = within(block, peers, own_y, wide_y)
        for at, (field, weight) in enumerate(planes_of(ref, spread, own_x, extent_z, wide_y)):
            weight = jnp.where(inside, weight, 0.0)
            cond[block * own_x + at] = weight
            even[block * own_x + at] = weight * field
    for power in range(STEPS):
        for at in range(power, own_x - power):
            basis_ref[power, at] = own_basis[power, at]

    def weight_of(x_at):
        return own_cond[x_at - own_x] if own_x <= x_at < 2 * own_x else cond[x_at]

    for power in range(1, POWERS + 1):

        def get(x_at, power=power):
            if known(power - 1, x_at):
                return own_scaled[power - 1, x_at - own_x]
            return slots[(power - 1) % 2][x_at]

        def put(x_at, value, scaled, power=power):
            if own_x <= x_at < 2 * own_x:
                basis_ref[power, x_at - own_x] = value[HALO : HALO + own_y]
            if power < POWERS:
                slots[power % 2][x_at] = scaled

        missing = [x_at for x_at in range(power, wide_x - power) if not known(power, x_at)]
        cuts = [at for at in range(1, len(missing)) if missing[at] != missing[at - 1] + 1]
        for first, last in zip([0] + cuts, cuts + [len(missing)]):
            for x_from, x_to in spans(missing[first], missing[last - 1] + 1):
                apply(used, wide_y, matrix, x_from, x_to, get, weight_of, put)

    def add(x_at, sums):
        for tile in range(own_y // 8):
            tiles = [basis_ref[power, x_at, tile * 8 : (tile + 1) * 8, :] for power in range(POWERS + 1)]
            sums = tuple(total + tiles[i] * tiles[j] for total, (i, j) in zip(sums, PAIRS))
        return sums

    sums = lax.fori_loop(0, own_x, add, tuple(jnp.zeros((8, LANES), F32) for _ in PAIRS))
    lines = [jnp.sum(total, axis=0, keepdims=True) for total in sums]
    lines.append(jnp.zeros((LANES - len(PAIRS), LANES), F32))
    table = jnp.concatenate(lines, axis=0)
    line = lax.dot_general(
        jnp.ones((8, LANES), F32),
        table,
        (((1,), (1,)), ((), ())),
        precision=lax.Precision.HIGHEST,
        preferred_element_type=F32,
    )[:1]
    gram_ref[...] = line


def spans(start, stop):
    count = -(-(stop - start) // CHUNK)
    marks = [start + (stop - start) * at // count for at in range(count + 1)]
    return list(zip(marks[:-1], marks[1:]))


def solve(gram):
    paired = [[gram[i][j] + gram[i + 1][j] for j in range(STEPS + 1)] for i in range(STEPS)]
    normal = [[paired[i][j] + paired[i][j + 1] for j in range(STEPS)] for i in range(STEPS)]
    target = [paired[i][0] for i in range(STEPS)]
    lower = [[None] * STEPS for _ in range(STEPS)]
    inverse = []
    for col in range(STEPS):
        value = normal[col][col]
        for k in range(col):
            value = value - lower[col][k] * lower[col][k]
        root = jnp.sqrt(value)
        lower[col][col] = root
        inverse.append(1.0 / root)
        for row in range(col + 1, STEPS):
            value = normal[row][col]
            for k in range(col):
                value = value - lower[row][k] * lower[col][k]
            lower[row][col] = value * inverse[col]
    forward = []
    for row in range(STEPS):
        value = target[row]
        for col in range(row):
            value = value - lower[row][col] * forward[col]
        forward.append(value * inverse[row])
    coefs = [None] * STEPS
    for row in range(STEPS - 1, -1, -1):
        value = forward[row]
        for col in range(row + 1, STEPS):
            value = value - lower[col][row] * coefs[col]
        coefs[row] = value * inverse[row]
    return coefs


def remainder(coefs):
    inner = [-(coefs[k - 1] + coefs[k]) for k in range(1, STEPS)]
    return [1.0 - coefs[0]] + inner + [-coefs[STEPS - 1]]


def turn_kernel(peers, basis_ref, out_ref, turned):
    _, own_x, _, _ = basis_ref.shape
    extent_z = out_ref.shape[2] // (own_x * VARS)
    for pair in range(POWERS // 2):
        for x_at in range(own_x):
            both = jnp.concatenate([basis_ref[2 * pair + 1, x_at], basis_ref[2 * pair + 2, x_at]], axis=0)
            turned[pair, x_at] = both.T
            for peer in range(peers):
                for var in range(VARS):
                    source = (var * peers + peer) * extent_z
                    place = (x_at * VARS + var) * extent_z
                    out_ref[peer, pair, place : place + extent_z, :] = turned[
                        pair, x_at, source : source + extent_z, :
                    ]


def finish_kernel(grams_ref, first_ref, *refs):
    parts, (solution_ref, residual_ref, solutions, residuals) = refs[:-4], refs[-4:]
    peers = len(parts)
    _, extent_x, extent_z, extent_y = first_ref.shape
    line = jnp.sum(grams_ref[...], axis=0)
    where = lane_iota(1)
    entry = {}
    for at, (i, j) in enumerate(PAIRS):
        value = jnp.sum(jnp.where(where == at, line, 0.0), axis=1, keepdims=True)
        entry[i, j] = entry[j, i] = value
    first = solve([[entry[i, j] for j in range(STEPS + 1)] for i in range(STEPS + 1)])
    left = remainder(first)
    half = {}
    for i in range(STEPS + 1):
        for j in range(POWERS + 1):
            value = left[0] * entry[i, j]
            for k in range(1, STEPS + 1):
                value = value + left[k] * entry[i + k, j]
            half[i, j] = value
    second_gram = []
    for i in range(STEPS + 1):
        line = []
        for j in range(STEPS + 1):
            value = left[0] * half[i, j]
            for k in range(1, STEPS + 1):
                value = value + left[k] * half[i, j + k]
            line.append(value)
        second_gram.append(line)
    second = solve(second_gram)
    last = remainder(second)
    of_solution = list(first) + [0.0] * STEPS
    of_residual = [0.0] * (POWERS + 1)
    for i in range(STEPS):
        for k in range(STEPS + 1):
            of_solution[i + k] = of_solution[i + k] + second[i] * left[k]
    for i in range(STEPS + 1):
        for k in range(STEPS + 1):
            of_residual[i + k] = of_residual[i + k] + last[i] * left[k]
    of_solution.append(0.0)
    middle = LANES // 2
    pick = lane_iota(1) < middle

    def paired(coefs, pair):
        return jnp.where(pick, coefs[2 * pair + 1], coefs[2 * pair + 2])

    at_z = lax.axis_index("gz")
    for shift, ref in enumerate(parts):
        chunk = lax.rem(at_z + peers - shift, peers)
        for coefs, sums in ((of_solution, solutions), (of_residual, residuals)):
            total = paired(coefs, 0) * ref[0]
            for pair in range(1, POWERS // 2):
                total = total + paired(coefs, pair) * ref[pair]
            sums[chunk] = total + roll_lanes(total, middle)
    lanes = lane_iota(extent_z)
    for x_at in range(extent_x):
        for var in range(VARS):
            place = (x_at * VARS + var) * extent_z
            rows = slice(place, place + extent_z)
            for tile in range(extent_y // LANES):
                columns = slice(tile * LANES, (tile + 1) * LANES)
                first_part = first_ref[var, x_at, :, columns]
                for coefs, sums, ref in (
                    (of_solution, solutions, solution_ref),
                    (of_residual, residuals, residual_ref),
                ):
                    rest = jnp.where(lanes < middle, sums[2 * tile, rows, :], sums[2 * tile + 1, rows, :])
                    ref[var, x_at, :, columns] = coefs[0] * first_part + rest


def call(kernel, out_shape, scratch=(), **more):
    return pl.pallas_call(
        kernel,
        out_shape=out_shape,
        scratch_shapes=scratch,
        compiler_params=pltpu.CompilerParams(vmem_limit_bytes=VMEM),
        **more,
    )


def ring(count):
    up = [(i, (i + 1) % count) for i in range(count)]
    return up, [(j, i) for i, j in up]


def per_device(right_side, conductance, blocks):
    count_x, count_y, count_z = (lax.axis_size(axis) for axis in ("gx", "gy", "gz"))
    _, extent_x, extent_z, extent_y = right_side.shape
    size_z = extent_z * count_z
    own_y = extent_y // count_z
    wide_y = own_y + 2 * HALO

    edge = jax.ShapeDtypeStruct((2, HALO, LANES), F32)
    strips, first, last = call(
        functools.partial(pack_kernel, count_z),
        (jax.ShapeDtypeStruct((count_z, wide_y + wide_y // 2, LANES), F32), edge, edge),
        (pltpu.VMEM((2 * LANES, extent_y), F32),),
    )(jnp.concatenate([right_side, conductance[None]], axis=0))
    up, down = ring(count_y)
    left = lax.ppermute(last, "gy", up)
    right = lax.ppermute(first, "gy", down)
    strips = call(
        functools.partial(edge_kernel, wide_y), jax.ShapeDtypeStruct(strips.shape, F32)
    )(strips, left, right)
    here = lax.all_to_all(strips, "gz", 0, 0, tiled=True)
    up, down = ring(count_x)
    before = lax.ppermute(here, "gx", up)
    after = lax.ppermute(here, "gx", down)

    rows = jnp.repeat(blocks.transpose(0, 2, 1).reshape(-1, VARS), size_z, axis=1)
    rows = jnp.pad(rows, ((0, 1), (0, LANES - VARS * size_z)))
    spread, matrix = call(
        functools.partial(matrix_kernel, count_z, extent_z),
        (
            jax.ShapeDtypeStruct((3 * LANES, 2 * LANES), BF16),
            jax.ShapeDtypeStruct((6 * LANES, 2 * LANES), BF16),
        ),
    )(rows)
    own = call(
        functools.partial(own_kernel, extent_x, extent_z),
        (
            jax.ShapeDtypeStruct((extent_x, wide_y, LANES), F32),
            jax.ShapeDtypeStruct((STEPS, extent_x, wide_y, LANES), F32),
            jax.ShapeDtypeStruct((STEPS, extent_x, own_y, LANES), F32),
        ),
    )(here, spread, matrix)
    planes = pltpu.VMEM((3 * extent_x, wide_y, LANES), F32)
    basis, gram = call(
        functools.partial(powers_kernel, extent_x, extent_z),
        (
            jax.ShapeDtypeStruct((POWERS + 1, extent_x, own_y, LANES), F32),
            jax.ShapeDtypeStruct((1, LANES), F32),
        ),
        (planes, planes, planes),
    )(before, after, *own, spread, matrix)

    pairs = [(i, i ^ 1) for i in range(count_y)]
    gram = gram + lax.ppermute(gram, "gy", pairs)
    chips = count_x * count_y * count_z // 2
    groups = [
        [(x * count_y + y) * count_z + z for x in range(count_x) for y in range(core, count_y, 2) for z in range(count_z)]
        for core in range(2)
    ]
    grams = jnp.broadcast_to(gram[None], (chips, 1, LANES))
    grams = lax.all_to_all(grams, ("gx", "gy", "gz"), 0, 0, tiled=True, axis_index_groups=groups)

    turned = call(
        functools.partial(turn_kernel, count_z),
        jax.ShapeDtypeStruct((count_z, POWERS // 2, extent_x * VARS * extent_z, LANES), F32),
        (pltpu.VMEM((POWERS // 2, extent_x, LANES, LANES), F32),),
    )(basis)
    at_z = lax.axis_index("gz")
    parts = []
    for shift in range(count_z):
        part = lax.dynamic_index_in_dim(turned, (at_z + shift) % count_z, 0, keepdims=False)
        if shift > 0:
            part = lax.ppermute(part, "gz", [(i, (i + shift) % count_z) for i in range(count_z)])
        parts.append(part)
    shape = jax.ShapeDtypeStruct(right_side.shape, F32)
    scratch = pltpu.VMEM((count_z, extent_x * VARS * extent_z, LANES), F32)
    return call(finish_kernel, (shape, shape), (scratch, scratch))(grams, right_side, *parts)


def solution(mesh):
    in_specs = (P(None, "gx", "gz", "gy"), P("gx", "gz", "gy"), P())
    out_specs = (P(None, "gx", "gz", "gy"), P(None, "gx", "gz", "gy"))
    return jax.shard_map(
        per_device, mesh=mesh, in_specs=in_specs, out_specs=out_specs, check_vma=False
    )
```
